128 devices in a mesh: row: 8 (over x, z_hi), col: 16 (over y, z_lo, core).
Axes of the slice: x: 4, y: 4, z: 4 (z_hi: 2, z_lo: 2; z = z_hi * 2 + z_lo), core: 2. Of those that a mesh axis runs over, the one named last changes fastest.
Arguments:
- a_tiles: bfloat16 [256, 16, 128, 128], P('col', 'row'), may hold values from -6 to 6
- a_cols: int32 [256, 16], P('col', 'row'), may hold values from 0 to 223, as said below
- b_tiles: bfloat16 [1792, 48, 128, 128], P('row', 'col'), may hold values from -0.5 to 0.5
- b_cols: int32 [1792, 48], P('row', 'col'), may hold values from 0 to 111, as said below
- c_cols: int32 [256, 32], P(None, 'col'), may hold values from 0 to 111, as said below
- keep: int32 [256, 16, 48], P(None, 'row', 'col'), may hold values from 0 to 1, as said below
Outputs:
- c_tiles: bfloat16 [256, 32, 128, 128], P('row', 'col')
The draws below stay inside these ranges and needn't reach their ends.
Inputs may be any that keep to these rules, and one draw needn't show every extreme that they name: Within one row of a_cols, the 2 entries of one inner panel are distinct. Within one row of b_cols, the 3 entries of one column panel are distinct. Within one row of c_cols, the 2 entries of one column panel are distinct. `keep`: take the 16 rows p * 16 to p * 16 + 15, the 2 entries r * 2 to r * 2 + 1 of the second dimension and the 3 entries c * 3 to c * 3 + 2 of the third: such a block holds at most 72 ones, and in every draw there is some pair (r, c) for which all 16 such blocks hold exactly 72.
All inputs are finite; a program needn't handle non-finite values.
Results may differ from the reference program's by a relative error of at most 0.011.
Values may be sent and summed in bfloat16 or wider, within the bound.
A program may use at most 320 MiB of HBM per device.

```python
import jax
import jax.numpy as jnp
from jax import lax

T_SIZE = 128
KB = 1792
SA = 2
SB = 3
SC = 2
PIECE = 16
MB = 256
KP = 224
JP = 112
CAP = 72
N_ROW = 8
N_COL = 16


def row_offsets(key):
    return jax.random.randint(jax.random.fold_in(key, 101), (MB,), 0, KP)


def distinct_picks(key, shape, choices_count, picks):
    scores = jax.random.randint(key, shape + (choices_count,), 0, 100000) * choices_count + jnp.arange(choices_count, dtype=jnp.int32)
    return jnp.argsort(scores, axis=-1)[..., :picks].astype(jnp.int32)


def draw_a_cols(key, part):
    offsets = row_offsets(key)
    key = jax.random.fold_in(key, 1)
    deltas = distinct_picks(key, (MB, N_ROW), 3, SA)
    result = (offsets[:, None, None] + deltas) % KP
    return result.reshape(MB, N_ROW * SA).astype(jnp.int32)


def draw_b_cols(key, part):
    key = jax.random.fold_in(key, 2)
    extra = distinct_picks(key, (KB, N_COL), 4, SB)
    rows = jnp.arange(KB, dtype=jnp.int32)
    result = (rows[:, None, None] + extra) % JP
    return result.reshape(KB, N_COL * SB).astype(jnp.int32)


def draw_c_cols(key, part):
    offsets = row_offsets(key)
    key = jax.random.fold_in(key, 3)
    extra = distinct_picks(key, (MB, N_COL), 6, SC)
    result = (offsets[:, None, None] + extra) % JP
    return result.reshape(MB, N_COL * SC).astype(jnp.int32)


def draw_keep(key, part):
    key = jax.random.fold_in(key, 4)
    key_busy, key_first, key_count, key_rank = jax.random.split(key, 4)
    cells = PIECE * SA * SB
    busy = jax.random.randint(key_busy, (N_ROW, N_COL), 0, 8) == 0
    chosen = jax.random.randint(key_first, (2,), 0, 100000)
    forced = (jnp.arange(N_ROW)[:, None] == chosen[0] % N_ROW) & (jnp.arange(N_COL)[None, :] == chosen[1] % N_COL)
    busy = busy | forced
    light = jax.random.randint(key_count, (N_COL, N_ROW, N_COL), CAP // 4, CAP // 3 + 1)
    counts = jnp.where(busy[None, :, :], CAP, light)
    scores = jax.random.randint(key_rank, (N_COL, N_ROW, N_COL, cells), 0, 1 << 20) * cells + jnp.arange(cells, dtype=jnp.int32)
    ranks = jnp.argsort(jnp.argsort(scores, axis=-1), axis=-1)
    blocks = (ranks < counts[..., None]).astype(jnp.int32)
    blocks = blocks.reshape(N_COL, N_ROW, N_COL, PIECE, SA, SB).transpose(0, 3, 1, 4, 2, 5)
    return blocks.reshape(MB, N_ROW * SA, N_COL * SB)


def shard_levels(rng, extent, shards, smallest, high):
    def one(dim, blocks):
        heights = jax.random.uniform(jax.random.fold_in(jax.random.fold_in(rng, 6), dim), (blocks,), jnp.float32, smallest / len(shards), high / len(shards))
        return jnp.repeat(jnp.exp(heights), extent[dim] // blocks).reshape((-1,) + (1,) * (len(extent) - dim - 1))

    gain = one(*shards[0])
    for cut in shards[1:]:
        gain = gain * one(*cut)
    return gain


def normal_values(own_key, extent, width, most, shards=(), kind=jnp.bfloat16):
    gain = shard_levels(own_key, extent, shards, -0.22, 0.18) if shards else 1.0
    array = jax.random.normal(own_key, extent, jnp.float32) * width * gain
    return jnp.minimum(jnp.maximum(array, -most), most).astype(kind)


def setup_inputs(seed: int = 0) -> dict:
    key_of = jax.random.split(jax.random.key(seed), 7)
    return {
        "a_tiles": normal_values(key_of[0], (MB, N_ROW * SA, T_SIZE, T_SIZE), 1.0, 6.0, ((0, 16), (1, 8))),
        "a_cols": draw_a_cols(jax.random.fold_in(key_of[6], 71), 0),
        "b_tiles": normal_values(key_of[2], (KB, N_COL * SB, T_SIZE, T_SIZE), T_SIZE ** -0.5, 0.5, ((0, 8), (1, 16))),
        "b_cols": draw_b_cols(jax.random.fold_in(key_of[6], 71), 0),
        "c_cols": draw_c_cols(jax.random.fold_in(key_of[6], 71), 0),
        "keep": draw_keep(jax.random.fold_in(key_of[6], 71), 0),
    }


def reference(a_tiles, a_cols, b_tiles, b_cols, c_cols, keep):
    a_split = a_tiles.reshape(MB, N_ROW, SA, T_SIZE, T_SIZE).transpose(1, 0, 2, 3, 4)
    a_index = a_cols.reshape(MB, N_ROW, SA).transpose(1, 0, 2)
    b_split = b_tiles.reshape(N_ROW, KP, N_COL, SB, T_SIZE, T_SIZE)
    b_index = b_cols.reshape(N_ROW, KP, N_COL, SB)
    c_index = c_cols.reshape(MB, N_COL, SC)
    keep_split = keep.reshape(MB, N_ROW, SA, N_COL, SB).transpose(1, 0, 2, 3, 4)

    def panel(running, inputs):
        a_panel, a_panel_index, b_panel, b_panel_index, keep_panel = inputs

        def one_row(row_inputs):
            a_row, row_index, c_row, keep_row = row_inputs
            right = b_panel[row_index.astype(jnp.int32)]
            target = b_panel_index[row_index.astype(jnp.int32)]
            weight = ((target[..., None] == c_row[None, :, None, :]) & (keep_row[..., None] == 1)).astype(jnp.float32)
            mixed = jnp.einsum("sctu,sctjk->scujk", weight, right.astype(jnp.float32))
            return jnp.einsum("sij,scujk->cuik", a_row.astype(jnp.float32), mixed)

        share = lax.map(one_row, (a_panel, a_panel_index, c_index, keep_panel))
        share = lax.optimization_barrier(share.astype(jnp.bfloat16))
        return running + share.astype(jnp.float32), None

    running = jnp.zeros((MB, N_COL, SC, T_SIZE, T_SIZE), jnp.float32)
    running, unused = lax.scan(panel, running, (a_split, a_index, b_split, b_index, keep_split))
    return running.astype(jnp.bfloat16).reshape(MB, N_COL * SC, T_SIZE, T_SIZE)
```

```python
import jax
import jax.numpy as jnp
from jax import lax
from jax.experimental import pallas as pl
from jax.experimental.pallas import tpu as pltpu
from jax.sharding import PartitionSpec as P

MESH = pl.DeviceIdType.MESH
T = 128
ROWS = 16
NC = 8
NR = ROWS // NC
KP = 224
SB = 3
BLOCKS = KP * SB
B_PARTS = 8


def kernel(
    meta_ref, a_ref, b_ref, out_ref,
    w, bv, rf, rd, rz, rzz, land, cols_v, meta_s, cols_s,
    sem_a, sem_f, sem_d, sem_z, sem_zz, sem_m, sem_b, sem_own, sem_s, sem_out, send_a, send_p, send_m,
):
    row, col = lax.axis_index("row"), lax.axis_index("col")
    x, zh = row // 2, row % 2
    y, zl, k = col // 4, (col // 2) % 2, col % 2
    yp, ym, y2 = (y + 1) % 4, (y + 3) % 4, (y + 2) % 4

    def dev(xx, hh, yy, ll, kk):
        return (xx * 2 + hh, yy * 4 + ll * 2 + kk)

    sibling = dev(x, zh, y, zl, 1 - k)
    z_near = dev(x, zh, y, 1 - zl, k)
    z_far = dev(x, 1 - zh, y, zl, k)
    y_up, y_down = dev(x, zh, yp, zl, k), dev(x, zh, ym, zl, k)

    def x_dev(xx):
        return dev(xx, zh, y, zl, k)

    def remote(src, dst, send, recv, device):
        return pltpu.make_async_remote_copy(
            src_ref=src, dst_ref=dst, send_sem=send, recv_sem=recv, device_id=device, device_id_type=MESH
        )

    def landed(dst, recv):
        remote(dst, dst, send_p, recv, sibling).wait_recv()

    def chunk(slot, c):
        return w.at[slot, pl.ds(c * NR, NR)]

    part = BLOCKS // B_PARTS
    b_copies = [
        pltpu.make_async_copy(b_ref.at[pl.ds(i * part, part)], bv.at[pl.ds(i * part, part)], sem_b.at[i])
        for i in range(B_PARTS)
    ]
    q_own = y * 2 + zl
    own_copy = pltpu.make_async_copy(a_ref, w.at[q_own], sem_own)
    meta_copy = pltpu.make_async_copy(meta_ref, meta_s, sem_s)
    own_copy.start()
    meta_copy.start()
    for copy in b_copies:
        copy.start()

    barrier = pltpu.get_barrier_semaphore()
    for j in range(1, 16):
        pl.semaphore_signal(barrier, 1, device_id=(row, (col + j) % 16), device_id_type=MESH)
    for device in (x_dev((x + 1) % 4), x_dev((x + 3) % 4), z_far):
        pl.semaphore_signal(barrier, 1, device_id=device, device_id_type=MESH)
    bv[BLOCKS] = jnp.zeros((T, T), bv.dtype)
    pl.semaphore_wait(barrier, 18)

    def send_a_chunk(src, slot, c, device):
        remote(src, chunk(slot, c), send_a, sem_a.at[slot, c], device).start()

    def wait_a(slot, c):
        landed(chunk(slot, c), sem_a.at[slot, c])

    def hop0(c):
        src = a_ref.at[pl.ds(c * NR, NR)]
        send_a_chunk(src, q_own, c, y_up)
        send_a_chunk(src, q_own, c, y_down)
        send_a_chunk(src, q_own, c, z_near)
        send_a_chunk(src, 8 + q_own, c, sibling)

    def pass_on(slot, c, up=None, down=None):
        wait_a(slot, c)
        src = chunk(slot, c)
        if up is not None:
            @pl.when(up)
            def _():
                send_a_chunk(src, slot, c, y_up)
        if down is not None:
            @pl.when(down)
            def _():
                send_a_chunk(src, slot, c, y_down)
        send_a_chunk(src, 8 + slot, c, sibling)

    def hop1(c):
        slot = y * 2 + 1 - zl
        pass_on(ym * 2 + zl, c, up=c % 2 == 0)
        pass_on(yp * 2 + zl, c, down=c % 2 == 1)
        wait_a(slot, c)
        src = chunk(slot, c)
        send_a_chunk(src, slot, c, y_up)
        send_a_chunk(src, slot, c, y_down)
        send_a_chunk(src, 8 + slot, c, sibling)

    def hop2(c):
        pass_on(ym * 2 + 1 - zl, c, up=c % 2 == 0)
        pass_on(yp * 2 + 1 - zl, c, down=c % 2 == 1)
        pass_on(y2 * 2 + zl, c)

    def hop3(c):
        pass_on(y2 * 2 + 1 - zl, c)

    def z_first(c, kk):
        return (c + kk) % 4 == 0

    def way(c):
        return 1 + 2 * (c % 2)

    def p_slot(yy, ll, kk):
        same = 1 - (kk + k) % 2
        return yy * 2 + ll + 8 + 8 * same

    def r_slot(ll, kk, c):
        return (ll * 2 + kk) * NC + c

    def zz_slot(xx, kk, c):
        return xx * 4 + kk * 2 + c // 4

    def send_x(xx, ll, kk, c):
        src = chunk(p_slot(xx, ll, kk), c)
        rel = ((xx - x + 4) * way(c)) % 4
        slot = r_slot(ll, kk, c)

        @pl.when(rel == 2)
        def _():
            remote(src, rf.at[slot], send_p, sem_f.at[slot], x_dev((x + way(c)) % 4)).start()

        @pl.when(rel == 3)
        def _():
            remote(src, rd.at[1, slot], send_p, sem_d.at[1, slot], x_dev((x + 4 - way(c)) % 4)).start()

    def add_into(slot, c, *others):
        for r in range(NR):
            for u in range(2):
                total = w[slot, c * NR + r, u].astype(jnp.float32)
                for ref, index in others:
                    total = total + ref[(*index, r, u)].astype(jnp.float32)
                w[slot, c * NR + r, u] = total.astype(w.dtype)

    def multiply(yy, ll, c):
        def one(dk, carry):
            kk = (k + dk) % 2
            q = yy * 2 + ll
            a_slot, out_slot = q + 8 * dk, q + 16 - 8 * dk

            @pl.when(dk == 1)
            def _():
                wait_a(a_slot, c)

            piece = yy * 4 + ll * 2 + kk
            for r in range(NR):
                local = c * NR + r
                right = []
                for s in range(2):
                    at = cols_s[piece, local * 2 + s]
                    b_word = meta_s[1 + lax.shift_right_logical(at, 7), at & 127]
                    e = (piece * ROWS + local) * 2 + s
                    c_word = meta_s[3 + e // 128, e % 128]
                    pair = []
                    for u in range(2):
                        goal = lax.shift_right_logical(c_word, 7 * u) & 127
                        which = jnp.int32(BLOCKS)
                        for t in range(SB):
                            there = lax.shift_right_logical(b_word, 7 * t) & 127
                            kept = lax.shift_right_logical(c_word, 14 + t) & 1
                            which = jnp.where((there == goal) & (kept == 1), at * SB + t, which)
                        pair.append(bv[which])
                    right.append(jnp.concatenate(pair, axis=1))
                left = jnp.concatenate([w[a_slot, local, 0], w[a_slot, local, 1]], axis=1)
                product = jnp.dot(left, jnp.concatenate(right, axis=0), preferred_element_type=jnp.float32)
                w[out_slot, local, 0] = product[:, :T].astype(w.dtype)
                w[out_slot, local, 1] = product[:, T:].astype(w.dtype)

            first = z_first(c, kk)

            @pl.when(jnp.logical_not(first))
            def _():
                send_x(yy, ll, kk, c)

            @pl.when(first & (ll != zh))
            def _():
                slot = zz_slot(yy, kk, c)
                remote(chunk(out_slot, c), rzz.at[slot], send_p, sem_zz.at[slot], z_far).start()

            return carry

        lax.fori_loop(0, 2, one, 0)

    def z_sum(c):
        for kk in range(2):
            @pl.when(z_first(c, kk))
            def _():
                def one(j, carry):
                    xx = (x + 2 + j) % 4
                    slot = zz_slot(xx, kk, c)
                    landed(rzz.at[slot], sem_zz.at[slot])
                    add_into(p_slot(xx, zh, kk), c, (rzz, (slot,)))
                    send_x(xx, zh, kk, c)
                    return carry

                lax.fori_loop(0, 4, one, 0)

    def middle(c, ll, kk):
        xx = (x + way(c)) % 4
        slot, own = r_slot(ll, kk, c), p_slot(xx, ll, kk)
        landed(rf.at[slot], sem_f.at[slot])
        add_into(own, c, (rf, (slot,)))
        remote(chunk(own, c), rd.at[0, slot], send_p, sem_d.at[0, slot], x_dev(xx)).start()

    def arrived(ll, kk, c):
        slot = r_slot(ll, kk, c)
        for side in range(2):
            landed(rd.at[side, slot], sem_d.at[side, slot])
        return (rd, (0, slot)), (rd, (1, slot))

    def write_out(own, kk, c):
        pltpu.make_async_copy(chunk(own, c), out_ref.at[pl.ds(kk * ROWS + c * NR, NR)], sem_out).start()

    def middles(c, only_z_first):
        for j in range(2):
            ll = (zl + j) % 2
            for kk in range(2):
                if only_z_first:
                    go = z_first(c, kk) & (ll == zh)
                else:
                    go = jnp.logical_not(z_first(c, kk))

                @pl.when(go)
                def _():
                    middle(c, ll, kk)

    def to_far(c):
        for kk in range(2):
            @pl.when(jnp.logical_not(z_first(c, kk)))
            def _():
                own = p_slot(x, 1 - zh, kk)
                add_into(own, c, *arrived(1 - zh, kk, c))
                slot = kk * NC + c
                remote(chunk(own, c), rz.at[slot], send_p, sem_z.at[slot], z_far).start()

    def finish(c):
        for kk in range(2):
            own = p_slot(x, zh, kk)
            slot = kk * NC + c

            @pl.when(z_first(c, kk))
            def _():
                add_into(own, c, *arrived(zh, kk, c))
                write_out(own, kk, c)

            @pl.when(jnp.logical_not(z_first(c, kk)))
            def _():
                both = arrived(zh, kk, c)
                landed(rz.at[slot], sem_z.at[slot])
                add_into(own, c, *both, (rz, (slot,)))
                write_out(own, kk, c)

    hop0(0)
    meta_copy.wait()
    for j in range(1, 16):
        remote(meta_ref, land.at[col], send_m, sem_m.at[col], (row, (col + j) % 16)).start()
    land[col] = meta_ref[...]
    hop1(0)
    for j in range(1, 16):
        other = (col + j) % 16
        landed(land.at[other], sem_m.at[other])
    cols_v[...] = land[:, 0, :]
    cols_copy = pltpu.make_async_copy(cols_v, cols_s, sem_s)
    cols_copy.start()
    cols_copy.wait()
    own_copy.wait()
    for copy in b_copies:
        copy.wait()

    def turn(c, carry):
        now, more = c < NC, c < NC - 1

        @pl.when(now)
        def _():
            multiply(y, zl, c)
            hop2(c)

        @pl.when(more)
        def _():
            hop0(c + 1)

        @pl.when(now)
        def _():
            multiply(ym, zl, c)
            multiply(yp, zl, c)
            multiply(y, 1 - zl, c)

        @pl.when((c >= 1) & (c < NC + 1))
        def _():
            z_sum(c - 1)
            middles(c - 1, False)

        @pl.when((c >= 2) & (c < NC + 2))
        def _():
            middles(c - 2, True)

        @pl.when(now)
        def _():
            hop3(c)

        @pl.when(more)
        def _():
            hop1(c + 1)

        @pl.when(now)
        def _():
            multiply(y2, zl, c)
            multiply(ym, 1 - zl, c)
            multiply(yp, 1 - zl, c)

        @pl.when((c >= 2) & (c < NC + 2))
        def _():
            to_far(c - 2)

        @pl.when(now)
        def _():
            multiply(y2, 1 - zl, c)

        @pl.when(c >= 3)
        def _():
            finish(c - 3)

        return carry

    lax.fori_loop(0, NC + 3, turn, 0)

    remote(w.at[pl.ds(0, 15)], w.at[pl.ds(0, 15)], send_a, send_a, sibling).wait_send()
    remote(w.at[pl.ds(0, 14)], w.at[pl.ds(0, 14)], send_p, send_p, sibling).wait_send()
    remote(land.at[pl.ds(0, 15)], land.at[pl.ds(0, 15)], send_m, send_m, sibling).wait_send()
    pltpu.make_async_copy(w.at[pl.ds(0, 2)], w.at[pl.ds(0, 2)], sem_out).wait()


def per_device(a_tiles, a_cols, b_tiles, b_cols, c_cols, keep):
    bf16, i32 = jnp.bfloat16, jnp.int32
    b_words = b_cols[:, 0] + 128 * b_cols[:, 1] + 16384 * b_cols[:, 2]
    kept = keep[:, :, 0] + 2 * keep[:, :, 1] + 4 * keep[:, :, 2]
    c_words = (c_cols[:, 0] + 128 * c_cols[:, 1])[:, None] + 16384 * kept
    meta = jnp.concatenate(
        [
            jnp.pad(a_cols.reshape(-1), (0, 128 - 2 * ROWS)),
            jnp.pad(b_words, (0, 256 - KP)),
            c_words.reshape(-1),
            jnp.zeros((128,), i32),
        ]
    ).reshape(8, 128)
    chunk = (NR, 2, T, T)
    vmem = pltpu.VMEM
    dma = pltpu.SemaphoreType.DMA
    return pl.pallas_call(
        kernel,
        out_shape=jax.ShapeDtypeStruct((2 * ROWS, 2, T, T), bf16),
        in_specs=[
            pl.BlockSpec(memory_space=pltpu.VMEM),
            pl.BlockSpec(memory_space=pl.ANY),
            pl.BlockSpec(memory_space=pl.ANY),
        ],
        out_specs=pl.BlockSpec(memory_space=pl.ANY),
        scratch_shapes=[
            vmem((24, ROWS, 2, T, T), bf16),
            vmem((BLOCKS + 1, T, T), bf16),
            vmem((4 * NC, *chunk), bf16),
            vmem((2, 4 * NC, *chunk), bf16),
            vmem((2 * NC, *chunk), bf16),
            vmem((16, *chunk), bf16),
            vmem((16, 8, 128), i32),
            vmem((16, 128), i32),
            pltpu.SMEM((8, 128), i32),
            pltpu.SMEM((16, 128), i32),
            dma((16, NC)),
            dma((4 * NC,)),
            dma((2, 4 * NC)),
            dma((2 * NC,)),
            dma((16,)),
            dma((16,)),
            dma((B_PARTS,)),
            dma,
            dma,
            dma,
            dma,
            dma,
            dma,
        ],
        compiler_params=pltpu.CompilerParams(
            collective_id=0, has_side_effects=True, vmem_limit_bytes=63 << 20
        ),
        cost_estimate=pl.CostEstimate(
            flops=2 * 256 * 2 * T * 2 * T * T, bytes_accessed=26 << 20, transcendentals=0
        ),
    )(meta, a_tiles, b_tiles.reshape(BLOCKS, T, T))


def solution(mesh):
    placed = (
        P("col", "row", None, None),
        P("col", "row"),
        P("row", "col", None, None),
        P("row", "col"),
        P(None, "col"),
        P(None, "row", "col"),
    )
    return jax.shard_map(
        per_device,
        mesh=mesh,
        in_specs=placed,
        out_specs=P("row", "col", None, None),
        check_vma=False,
    )
```

```python
import jax
import jax.numpy as jnp
from jax import lax
from jax.experimental import pallas as pl
from jax.experimental.pallas import tpu as pltpu
from jax.sharding import PartitionSpec as P

MESH = pl.DeviceIdType.MESH
T = 128
ROWS = 16
NC = 16
NR = ROWS // NC
KP = 224
SB = 3
BLOCKS = KP * SB
B_PARTS = 8
Z_FIRST = 5


def kernel(
    meta_ref, a_ref, b_ref, out_ref,
    w, bv, rf, rd, rz, rzz, land, cols_v, meta_s, cols_s,
    sem_a, sem_f, sem_d, sem_z, sem_zz, sem_m, sem_b, sem_own, sem_s, sem_out, send_a, send_p, send_m,
):
    row, col = lax.axis_index("row"), lax.axis_index("col")
    x, zh = row // 2, row % 2
    y, zl, k = col // 4, (col // 2) % 2, col % 2
    yp, ym, y2 = (y + 1) % 4, (y + 3) % 4, (y + 2) % 4

    def dev(xx, hh, yy, ll, kk):
        return (xx * 2 + hh, yy * 4 + ll * 2 + kk)

    sibling = dev(x, zh, y, zl, 1 - k)
    z_near = dev(x, zh, y, 1 - zl, k)
    z_far = dev(x, 1 - zh, y, zl, k)
    y_up, y_down = dev(x, zh, yp, zl, k), dev(x, zh, ym, zl, k)

    def x_dev(xx):
        return dev(xx, zh, y, zl, k)

    def remote(src, dst, send, recv, device):
        return pltpu.make_async_remote_copy(
            src_ref=src, dst_ref=dst, send_sem=send, recv_sem=recv, device_id=device, device_id_type=MESH
        )

    def landed(dst, recv):
        remote(dst, dst, send_p, recv, sibling).wait_recv()

    def chunk(slot, c):
        return w.at[slot, pl.ds(c * NR, NR)]

    part = BLOCKS // B_PARTS
    b_copies = [
        pltpu.make_async_copy(b_ref.at[pl.ds(i * part, part)], bv.at[pl.ds(i * part, part)], sem_b.at[i])
        for i in range(B_PARTS)
    ]
    q_own = y * 2 + zl
    own_copy = pltpu.make_async_copy(a_ref, w.at[q_own], sem_own)
    meta_copy = pltpu.make_async_copy(meta_ref, meta_s, sem_s)
    own_copy.start()
    meta_copy.start()
    for copy in b_copies:
        copy.start()

    barrier = pltpu.get_barrier_semaphore()
    for j in range(1, 16):
        pl.semaphore_signal(barrier, 1, device_id=(row, (col + j) % 16), device_id_type=MESH)
    for device in (x_dev((x + 1) % 4), x_dev((x + 3) % 4), z_far):
        pl.semaphore_signal(barrier, 1, device_id=device, device_id_type=MESH)
    bv[BLOCKS] = jnp.zeros((T, T), bv.dtype)
    pl.semaphore_wait(barrier, 18)

    def send_a_chunk(src, slot, c, device):
        remote(src, chunk(slot, c), send_a, sem_a.at[slot, c], device).start()

    def wait_a(slot, c):
        landed(chunk(slot, c), sem_a.at[slot, c])

    def hop0(c):
        src = a_ref.at[pl.ds(c * NR, NR)]
        send_a_chunk(src, q_own, c, y_up)
        send_a_chunk(src, q_own, c, y_down)
        send_a_chunk(src, q_own, c, z_near)
        send_a_chunk(src, 8 + q_own, c, sibling)

    def pass_on(slot, c, up=None, down=None):
        wait_a(slot, c)
        src = chunk(slot, c)
        if up is not None:
            @pl.when(up)
            def _():
                send_a_chunk(src, slot, c, y_up)
        if down is not None:
            @pl.when(down)
            def _():
                send_a_chunk(src, slot, c, y_down)
        send_a_chunk(src, 8 + slot, c, sibling)

    def hop1(c):
        slot = y * 2 + 1 - zl
        pass_on(ym * 2 + zl, c, up=(c + k) % 2 == 0)
        pass_on(yp * 2 + zl, c, down=(c + k) % 2 == 1)
        wait_a(slot, c)
        src = chunk(slot, c)
        send_a_chunk(src, slot, c, y_up)
        send_a_chunk(src, slot, c, y_down)
        send_a_chunk(src, 8 + slot, c, sibling)

    def hop2(c):
        pass_on(ym * 2 + 1 - zl, c, up=(c + k) % 2 == 0)
        pass_on(yp * 2 + 1 - zl, c, down=(c + k) % 2 == 1)
        pass_on(y2 * 2 + zl, c)

    def hop3(c):
        pass_on(y2 * 2 + 1 - zl, c)

    def z_first(c, kk):
        return (c + 2 * kk) % 4 == 0

    def way(c, kk):
        return 1 + 2 * ((c + kk) % 2)

    def p_slot(yy, ll, kk):
        same = 1 - (kk + k) % 2
        return yy * 2 + ll + 8 + 8 * same

    def r_slot(ll, kk, c):
        return (ll * 2 + kk) * NC + c

    def zz_slot(xx, kk, c):
        return (xx * 2 + kk) * 4 + c // 4

    def send_x(xx, ll, kk, c):
        src = chunk(p_slot(xx, ll, kk), c)
        rel = ((xx - x + 4) * way(c, kk)) % 4
        slot = r_slot(ll, kk, c)

        @pl.when(rel == 2)
        def _():
            remote(src, rf.at[slot], send_p, sem_f.at[slot], x_dev((x + way(c, kk)) % 4)).start()

        @pl.when(rel == 3)
        def _():
            remote(src, rd.at[1, slot], send_p, sem_d.at[1, slot], x_dev((x + 4 - way(c, kk)) % 4)).start()

    def add_into(slot, c, *others):
        for r in range(NR):
            for u in range(2):
                total = w[slot, c * NR + r, u].astype(jnp.float32)
                for ref, index in others:
                    total = total + ref[(*index, r, u)].astype(jnp.float32)
                w[slot, c * NR + r, u] = total.astype(w.dtype)

    def multiply(c, *places):
        def one(dk, carry):
            kk = (k + dk) % 2
            slots = [(yy * 2 + ll + 8 * dk, yy * 2 + ll + 16 - 8 * dk) for yy, ll in places]

            @pl.when(dk == 1)
            def _():
                for a_slot, _ in slots:
                    wait_a(a_slot, c)

            rows = [c * NR + r for r in range(NR)]
            found = []
            for yy, ll in places:
                piece = yy * 4 + ll * 2 + kk
                for local in rows:
                    for s in range(2):
                        at = cols_s[piece, local * 2 + s]
                        b_word = meta_s[1 + lax.shift_right_logical(at, 7), at & 127]
                        e = (piece * ROWS + local) * 2 + s
                        c_word = meta_s[3 + e // 128, e % 128]
                        for u in range(2):
                            goal = lax.shift_right_logical(c_word, 7 * u) & 127
                            which = jnp.int32(BLOCKS)
                            for t in range(SB):
                                there = lax.shift_right_logical(b_word, 7 * t) & 127
                                kept = lax.shift_right_logical(c_word, 14 + t) & 1
                                which = jnp.where((there == goal) & (kept == 1), at * SB + t, which)
                            found.append(which)
            products = []
            for a_slot, _ in slots:
                for local in rows:
                    n = 4 * len(products)
                    right = [bv[which] for which in found[n : n + 4]]
                    right = [jnp.concatenate(right[i : i + 2], axis=1) for i in (0, 2)]
                    left = jnp.concatenate([w[a_slot, local, 0], w[a_slot, local, 1]], axis=1)
                    products.append(
                        jnp.dot(left, jnp.concatenate(right, axis=0), preferred_element_type=jnp.float32)
                    )
            for i, (_, out_slot) in enumerate(slots):
                for r, local in enumerate(rows):
                    product = products[i * NR + r]
                    w[out_slot, local, 0] = product[:, :T].astype(w.dtype)
                    w[out_slot, local, 1] = product[:, T:].astype(w.dtype)

            first = z_first(c, kk)

            @pl.when(jnp.logical_not(first))
            def _():
                for yy, ll in places:
                    send_x(yy, ll, kk, c)

            for (yy, ll), (_, out_slot) in zip(places, slots):

                @pl.when(first & (ll != zh))
                def _():
                    slot = zz_slot(yy, kk, c)
                    remote(chunk(out_slot, c), rzz.at[slot], send_p, sem_zz.at[slot], z_far).start()

            return carry

        lax.fori_loop(0, 2, one, 0)

    def z_sum(c):
        for kk in range(2):
            @pl.when(z_first(c, kk))
            def _():
                def one(j, carry):
                    xx = (x + 2 + j) % 4
                    slot = zz_slot(xx, kk, c)
                    landed(rzz.at[slot], sem_zz.at[slot])
                    add_into(p_slot(xx, zh, kk), c, (rzz, (slot,)))
                    send_x(xx, zh, kk, c)
                    return carry

                lax.fori_loop(0, 4, one, 0)

    def middle(c, ll, kk):
        xx = (x + way(c, kk)) % 4
        slot, own = r_slot(ll, kk, c), p_slot(xx, ll, kk)
        landed(rf.at[slot], sem_f.at[slot])
        add_into(own, c, (rf, (slot,)))
        remote(chunk(own, c), rd.at[0, slot], send_p, sem_d.at[0, slot], x_dev(xx)).start()

    def arrived(ll, kk, c):
        slot = r_slot(ll, kk, c)
        for side in range(2):
            landed(rd.at[side, slot], sem_d.at[side, slot])
        return (rd, (0, slot)), (rd, (1, slot))

    def write_out(own, kk, c):
        pltpu.make_async_copy(chunk(own, c), out_ref.at[pl.ds(kk * ROWS + c * NR, NR)], sem_out).start()

    def middles(c, only_z_first):
        for j in range(2):
            ll = (zl + j) % 2
            for kk in range(2):
                if only_z_first:
                    go = z_first(c, kk) & (ll == zh)
                else:
                    go = jnp.logical_not(z_first(c, kk))

                @pl.when(go)
                def _():
                    middle(c, ll, kk)

    def to_far(c):
        for kk in range(2):
            @pl.when(jnp.logical_not(z_first(c, kk)))
            def _():
                own = p_slot(x, 1 - zh, kk)
                add_into(own, c, *arrived(1 - zh, kk, c))
                slot = kk * NC + c
                remote(chunk(own, c), rz.at[slot], send_p, sem_z.at[slot], z_far).start()

    def finish(c):
        for kk in range(2):
            own = p_slot(x, zh, kk)
            slot = kk * NC + c

            @pl.when(z_first(c, kk))
            def _():
                add_into(own, c, *arrived(zh, kk, c))
                write_out(own, kk, c)

            @pl.when(jnp.logical_not(z_first(c, kk)))
            def _():
                both = arrived(zh, kk, c)
                landed(rz.at[slot], sem_z.at[slot])
                add_into(own, c, *both, (rz, (slot,)))
                write_out(own, kk, c)

    hop0(0)
    meta_copy.wait()
    for j in range(1, 16):
        remote(meta_ref, land.at[col], send_m, sem_m.at[col], (row, (col + j) % 16)).start()
    land[col] = meta_ref[...]
    hop0(1)
    hop1(0)
    for j in range(1, 16):
        other = (col + j) % 16
        landed(land.at[other], sem_m.at[other])
    cols_v[...] = land[:, 0, :]
    cols_copy = pltpu.make_async_copy(cols_v, cols_s, sem_s)
    cols_copy.start()
    cols_copy.wait()
    own_copy.wait()
    for copy in b_copies:
        copy.wait()

    def during(c, end):
        return pl.when((c >= 0) & (c < end))

    def turn(a, carry):
        @during(a, NC)
        def _():
            multiply(a, (y, zl))

        @during(a + 1, NC)
        def _():
            hop1(a + 1)

        @during(a, NC)
        def _():
            hop2(a)

        @during(a - 1, NC)
        def _():
            hop3(a - 1)

        @during(a + 2, NC)
        def _():
            hop0(a + 2)

        @during(a, NC)
        def _():
            multiply(a, (ym, zl), (yp, zl), (y, 1 - zl))

        @during(a - 2, NC)
        def _():
            z_sum(a - 2)
            middles(a - 2, False)

        @during(a - 3, NC)
        def _():
            middles(a - 3, True)

        @during(a, NC)
        def _():
            multiply(a, (y2, zl), (ym, 1 - zl), (yp, 1 - zl))

        @during(a - 1, NC)
        def _():
            multiply(a - 1, (y2, 1 - zl))

        @during(a - 3, NC)
        def _():
            to_far(a - 3)

        @during(a - 4, NC)
        def _():
            finish(a - 4)

        return carry

    lax.fori_loop(0, NC + 4, turn, 0)

    remote(w.at[pl.ds(0, 15)], w.at[pl.ds(0, 15)], send_a, send_a, sibling).wait_send()
    remote(w.at[pl.ds(0, 14)], w.at[pl.ds(0, 14)], send_p, send_p, sibling).wait_send()
    remote(land.at[pl.ds(0, 15)], land.at[pl.ds(0, 15)], send_m, send_m, sibling).wait_send()
    pltpu.make_async_copy(w.at[pl.ds(0, 2)], w.at[pl.ds(0, 2)], sem_out).wait()


def per_device(a_tiles, a_cols, b_tiles, b_cols, c_cols, keep):
    bf16, i32 = jnp.bfloat16, jnp.int32
    b_words = b_cols[:, 0] + 128 * b_cols[:, 1] + 16384 * b_cols[:, 2]
    kept = keep[:, :, 0] + 2 * keep[:, :, 1] + 4 * keep[:, :, 2]
    c_words = (c_cols[:, 0] + 128 * c_cols[:, 1])[:, None] + 16384 * kept
    meta = jnp.concatenate(
        [
            jnp.pad(a_cols.reshape(-1), (0, 128 - 2 * ROWS)),
            jnp.pad(b_words, (0, 256 - KP)),
            c_words.reshape(-1),
            jnp.zeros((128,), i32),
        ]
    ).reshape(8, 128)
    chunk = (NR, 2, T, T)
    vmem = pltpu.VMEM
    dma = pltpu.SemaphoreType.DMA
    return pl.pallas_call(
        kernel,
        out_shape=jax.ShapeDtypeStruct((2 * ROWS, 2, T, T), bf16),
        in_specs=[
            pl.BlockSpec(memory_space=pltpu.VMEM),
            pl.BlockSpec(memory_space=pl.ANY),
            pl.BlockSpec(memory_space=pl.ANY),
        ],
        out_specs=pl.BlockSpec(memory_space=pl.ANY),
        scratch_shapes=[
            vmem((24, ROWS, 2, T, T), bf16),
            vmem((BLOCKS + 1, T, T), bf16),
            vmem((4 * NC, *chunk), bf16),
            vmem((2, 4 * NC, *chunk), bf16),
            vmem((2 * NC, *chunk), bf16),
            vmem((8 * Z_FIRST, *chunk), bf16),
            vmem((16, 8, 128), i32),
            vmem((16, 128), i32),
            pltpu.SMEM((8, 128), i32),
            pltpu.SMEM((16, 128), i32),
            dma((16, NC)),
            dma((4 * NC,)),
            dma((2, 4 * NC)),
            dma((2 * NC,)),
            dma((8 * Z_FIRST,)),
            dma((16,)),
            dma((B_PARTS,)),
            dma,
            dma,
            dma,
            dma,
            dma,
            dma,
        ],
        compiler_params=pltpu.CompilerParams(
            collective_id=0, has_side_effects=True, vmem_limit_bytes=63 << 20
        ),
        cost_estimate=pl.CostEstimate(
            flops=2 * 256 * 2 * T * 2 * T * T, bytes_accessed=26 << 20, transcendentals=0
        ),
    )(meta, a_tiles, b_tiles.reshape(BLOCKS, T, T))


def solution(mesh):
    placed = (
        P("col", "row", None, None),
        P("col", "row"),
        P("row", "col", None, None),
        P("row", "col"),
        P(None, "col"),
        P(None, "row", "col"),
    )
    return jax.shard_map(
        per_device,
        mesh=mesh,
        in_specs=placed,
        out_specs=P("row", "col", None, None),
        check_vma=False,
    )
```

```python
import jax
import jax.numpy as jnp
from jax import lax
from jax.experimental import pallas as pl
from jax.experimental.pallas import tpu as pltpu
from jax.sharding import PartitionSpec as P

MESH = pl.DeviceIdType.MESH
T = 128
ROWS = 16
NC = 16
NR = ROWS // NC
KP = 224
SB = 3
BLOCKS = KP * SB
B_PARTS = 8


def kernel(
    a_cols_ref, b_cols_ref, c_cols_ref, keep_ref, a_ref, b_ref, out_ref,
    w, bv, rf, rd, rz, rzz, mine, land, cols_v, b_words, c_words, b_words_s, c_words_s, cols_s,
    sem_a, sem_f, sem_d, sem_z, sem_zz, sem_m, sem_b, sem_own, sem_words, sem_cols, sem_out, send_a, send_p, send_m,
):
    row, col = lax.axis_index("row"), lax.axis_index("col")
    x, zh = row // 2, row % 2
    y, zl, k = col // 4, (col // 2) % 2, col % 2
    yp, ym, y2 = (y + 1) % 4, (y + 3) % 4, (y + 2) % 4

    def dev(xx, hh, yy, ll, kk):
        return (xx * 2 + hh, yy * 4 + ll * 2 + kk)

    sibling = dev(x, zh, y, zl, 1 - k)
    z_near = dev(x, zh, y, 1 - zl, k)
    z_far = dev(x, 1 - zh, y, zl, k)
    y_up, y_down = dev(x, zh, yp, zl, k), dev(x, zh, ym, zl, k)

    def x_dev(xx):
        return dev(xx, zh, y, zl, k)

    def remote(src, dst, send, recv, device):
        return pltpu.make_async_remote_copy(
            src_ref=src, dst_ref=dst, send_sem=send, recv_sem=recv, device_id=device, device_id_type=MESH
        )

    def landed(dst, recv):
        remote(dst, dst, send_p, recv, sibling).wait_recv()

    def chunk(slot, c):
        return w.at[slot, pl.ds(c * NR, NR)]

    part = BLOCKS // B_PARTS
    b_copies = [
        pltpu.make_async_copy(b_ref.at[pl.ds(i * part, part)], bv.at[pl.ds(i * part, part)], sem_b.at[i])
        for i in range(B_PARTS)
    ]
    q_own = y * 2 + zl
    own_copy = pltpu.make_async_copy(a_ref, w.at[q_own], sem_own)
    for copy in b_copies:
        copy.start()
    own_copy.start()

    barrier = pltpu.get_barrier_semaphore()
    for j in range(1, 16):
        pl.semaphore_signal(barrier, 1, device_id=(row, (col + j) % 16), device_id_type=MESH)
    for device in (x_dev((x + 1) % 4), x_dev((x + 3) % 4), z_far):
        pl.semaphore_signal(barrier, 1, device_id=device, device_id_type=MESH)
    bv[BLOCKS] = jnp.zeros((T, T), bv.dtype)
    mine[...] = jnp.zeros_like(mine)
    mine[0:2, 0:ROWS] = a_cols_ref[...]
    b_words[0:1, 0:KP] = b_cols_ref[0:1] + 128 * b_cols_ref[1:2] + 16384 * b_cols_ref[2:3]
    c_words[...] = (
        c_cols_ref[0:1] + 128 * c_cols_ref[1:2] + 16384 * (keep_ref[0] + 2 * keep_ref[1] + 4 * keep_ref[2])
    )
    words_copies = [
        pltpu.make_async_copy(b_words, b_words_s, sem_words.at[0]),
        pltpu.make_async_copy(c_words, c_words_s, sem_words.at[1]),
    ]
    for copy in words_copies:
        copy.start()
    pl.semaphore_wait(barrier, 18)

    def send_a_chunk(src, slot, c, device):
        remote(src, chunk(slot, c), send_a, sem_a.at[slot, c], device).start()

    def wait_a(slot, c):
        landed(chunk(slot, c), sem_a.at[slot, c])

    def hop0(c):
        src = a_ref.at[pl.ds(c * NR, NR)]
        send_a_chunk(src, q_own, c, y_up)
        send_a_chunk(src, q_own, c, y_down)
        send_a_chunk(src, q_own, c, z_near)
        send_a_chunk(src, 8 + q_own, c, sibling)

    def pass_on(slot, c, up=None, down=None):
        wait_a(slot, c)
        src = chunk(slot, c)
        if up is not None:
            @pl.when(up)
            def _():
                send_a_chunk(src, slot, c, y_up)
        if down is not None:
            @pl.when(down)
            def _():
                send_a_chunk(src, slot, c, y_down)
        send_a_chunk(src, 8 + slot, c, sibling)

    def hop1(c):
        slot = y * 2 + 1 - zl
        pass_on(ym * 2 + zl, c, up=(c + k) % 2 == 0)
        pass_on(yp * 2 + zl, c, down=(c + k) % 2 == 1)
        wait_a(slot, c)
        src = chunk(slot, c)
        send_a_chunk(src, slot, c, y_up)
        send_a_chunk(src, slot, c, y_down)
        send_a_chunk(src, 8 + slot, c, sibling)

    def hop2(c):
        pass_on(ym * 2 + 1 - zl, c, up=(c + k) % 2 == 0)
        pass_on(yp * 2 + 1 - zl, c, down=(c + k) % 2 == 1)
        pass_on(y2 * 2 + zl, c)

    def hop3(c):
        pass_on(y2 * 2 + 1 - zl, c)

    def z_first(c, kk):
        return (c + 2 * kk) % 4 == 0

    def way(c, kk):
        return 1 + 2 * ((c + kk) % 2)

    def p_slot(yy, ll, kk):
        same = 1 - (kk + k) % 2
        return yy * 2 + ll + 8 + 8 * same

    def r_slot(ll, kk, c):
        return (ll * 2 + kk) * NC + c

    def zz_slot(xx, kk, c):
        return (xx * 2 + kk) * 4 + c // 4

    def send_x(xx, ll, kk, c):
        src = chunk(p_slot(xx, ll, kk), c)
        rel = ((xx - x + 4) * way(c, kk)) % 4
        slot = r_slot(ll, kk, c)

        @pl.when(rel == 2)
        def _():
            remote(src, rf.at[slot], send_p, sem_f.at[slot], x_dev((x + way(c, kk)) % 4)).start()

        @pl.when(rel == 3)
        def _():
            remote(src, rd.at[1, slot], send_p, sem_d.at[1, slot], x_dev((x + 4 - way(c, kk)) % 4)).start()

    def add_into(slot, c, *others):
        for r in range(NR):
            for u in range(2):
                total = w[slot, c * NR + r, u].astype(jnp.float32)
                for ref, index in others:
                    total = total + ref[(*index, r, u)].astype(jnp.float32)
                w[slot, c * NR + r, u] = total.astype(w.dtype)

    def multiply(c, *places):
        def one(dk, carry):
            kk = (k + dk) % 2
            slots = [(yy * 2 + ll + 8 * dk, yy * 2 + ll + 16 - 8 * dk) for yy, ll in places]

            @pl.when(dk == 1)
            def _():
                for a_slot, _ in slots:
                    wait_a(a_slot, c)

            rows = [c * NR + r for r in range(NR)]
            found = []
            for yy, ll in places:
                piece = yy * 4 + ll * 2 + kk
                for local in rows:
                    for s in range(2):
                        at = cols_s[16 * s + piece, local]
                        b_word = b_words_s[0, at]
                        c_word = c_words_s[s, piece * ROWS + local]
                        for u in range(2):
                            goal = lax.shift_right_logical(c_word, 7 * u) & 127
                            which = jnp.int32(BLOCKS)
                            for t in range(SB):
                                there = lax.shift_right_logical(b_word, 7 * t) & 127
                                kept = lax.shift_right_logical(c_word, 14 + t) & 1
                                which = jnp.where((there == goal) & (kept == 1), at * SB + t, which)
                            found.append(which)
            products = []
            for a_slot, _ in slots:
                for local in rows:
                    n = 4 * len(products)
                    right = [bv[which] for which in found[n : n + 4]]
                    right = [jnp.concatenate(right[i : i + 2], axis=1) for i in (0, 2)]
                    left = jnp.concatenate([w[a_slot, local, 0], w[a_slot, local, 1]], axis=1)
                    products.append(
                        jnp.dot(left, jnp.concatenate(right, axis=0), preferred_element_type=jnp.float32)
                    )
            for i, (_, out_slot) in enumerate(slots):
                for r, local in enumerate(rows):
                    product = products[i * NR + r]
                    w[out_slot, local, 0] = product[:, :T].astype(w.dtype)
                    w[out_slot, local, 1] = product[:, T:].astype(w.dtype)

            first = z_first(c, kk)

            @pl.when(jnp.logical_not(first))
            def _():
                for yy, ll in places:
                    send_x(yy, ll, kk, c)

            for (yy, ll), (_, out_slot) in zip(places, slots):

                @pl.when(first & (ll != zh))
                def _():
                    slot = zz_slot(yy, kk, c)
                    remote(chunk(out_slot, c), rzz.at[slot], send_p, sem_zz.at[slot], z_far).start()

            return carry

        lax.fori_loop(0, 2, one, 0)

    def z_sum(c):
        for kk in range(2):
            @pl.when(z_first(c, kk))
            def _():
                def one(j, carry):
                    xx = (x + 2 + j) % 4
                    slot = zz_slot(xx, kk, c)
                    landed(rzz.at[slot], sem_zz.at[slot])
                    add_into(p_slot(xx, zh, kk), c, (rzz, (slot,)))
                    send_x(xx, zh, kk, c)
                    return carry

                lax.fori_loop(0, 4, one, 0)

    def middle(c, ll, kk):
        xx = (x + way(c, kk)) % 4
        slot, own = r_slot(ll, kk, c), p_slot(xx, ll, kk)
        landed(rf.at[slot], sem_f.at[slot])
        add_into(own, c, (rf, (slot,)))
        remote(chunk(own, c), rd.at[0, slot], send_p, sem_d.at[0, slot], x_dev(xx)).start()

    def arrived(ll, kk, c):
        slot = r_slot(ll, kk, c)
        for side in range(2):
            landed(rd.at[side, slot], sem_d.at[side, slot])
        return (rd, (0, slot)), (rd, (1, slot))

    def write_out(own, kk, c):
        pltpu.make_async_copy(chunk(own, c), out_ref.at[pl.ds(kk * ROWS + c * NR, NR)], sem_out).start()

    def middles(c, only_z_first):
        for j in range(2):
            ll = (zl + j) % 2
            for kk in range(2):
                if only_z_first:
                    go = z_first(c, kk) & (ll == zh)
                else:
                    go = jnp.logical_not(z_first(c, kk))

                @pl.when(go)
                def _():
                    middle(c, ll, kk)

    def to_far(c):
        for kk in range(2):
            @pl.when(jnp.logical_not(z_first(c, kk)))
            def _():
                own = p_slot(x, 1 - zh, kk)
                add_into(own, c, *arrived(1 - zh, kk, c))
                slot = kk * NC + c
                remote(chunk(own, c), rz.at[slot], send_p, sem_z.at[slot], z_far).start()

    def finish(c):
        for kk in range(2):
            own = p_slot(x, zh, kk)
            slot = kk * NC + c

            @pl.when(z_first(c, kk))
            def _():
                add_into(own, c, *arrived(zh, kk, c))
                write_out(own, kk, c)

            @pl.when(jnp.logical_not(z_first(c, kk)))
            def _():
                both = arrived(zh, kk, c)
                landed(rz.at[slot], sem_z.at[slot])
                add_into(own, c, *both, (rz, (slot,)))
                write_out(own, kk, c)

    hop0(0)
    for j in range(1, 16):
        remote(mine, land.at[col], send_m, sem_m.at[col], (row, (col + j) % 16)).start()
    land[col] = mine[...]
    hop0(1)
    hop1(0)
    for j in range(1, 16):
        other = (col + j) % 16
        landed(land.at[other], sem_m.at[other])
    for s in range(2):
        cols_v[16 * s : 16 * s + 16] = land[:, s, :]
    cols_copy = pltpu.make_async_copy(cols_v, cols_s, sem_cols)
    cols_copy.start()
    for copy in (*words_copies, cols_copy):
        copy.wait()
    own_copy.wait()
    for copy in b_copies:
        copy.wait()

    def during(c, end):
        return pl.when((c >= 0) & (c < end))

    def turn(a, carry):
        @during(a, NC)
        def _():
            multiply(a, (y, zl))

        @during(a + 1, NC)
        def _():
            hop1(a + 1)

        @during(a, NC)
        def _():
            hop2(a)

        @during(a - 1, NC)
        def _():
            hop3(a - 1)

        @during(a + 2, NC)
        def _():
            hop0(a + 2)

        @during(a, NC)
        def _():
            multiply(a, (ym, zl), (yp, zl), (y, 1 - zl))

        @during(a - 2, NC)
        def _():
            z_sum(a - 2)
            middles(a - 2, False)

        @during(a - 3, NC)
        def _():
            middles(a - 3, True)

        @during(a, NC)
        def _():
            multiply(a, (y2, zl), (ym, 1 - zl), (yp, 1 - zl))

        @during(a - 1, NC)
        def _():
            multiply(a - 1, (y2, 1 - zl))

        @during(a - 3, NC)
        def _():
            to_far(a - 3)

        @during(a - 4, NC)
        def _():
            finish(a - 4)

        return carry

    lax.fori_loop(0, NC + 4, turn, 0)

    remote(w.at[pl.ds(0, 15)], w.at[pl.ds(0, 15)], send_a, send_a, sibling).wait_send()
    remote(w.at[pl.ds(0, 14)], w.at[pl.ds(0, 14)], send_p, send_p, sibling).wait_send()
    remote(land.at[pl.ds(0, 15)], land.at[pl.ds(0, 15)], send_m, send_m, sibling).wait_send()
    pltpu.make_async_copy(w.at[pl.ds(0, 2)], w.at[pl.ds(0, 2)], sem_out).wait()


def per_device(a_tiles, a_cols, b_tiles, b_cols, c_cols, keep):
    bf16, i32 = jnp.bfloat16, jnp.int32
    chunk = (NR, 2, T, T)
    vmem = pltpu.VMEM
    dma = pltpu.SemaphoreType.DMA
    return pl.pallas_call(
        kernel,
        out_shape=jax.ShapeDtypeStruct((2 * ROWS, 2, T, T), bf16),
        in_specs=[
            *[pl.BlockSpec(memory_space=pltpu.VMEM)] * 4,
            pl.BlockSpec(memory_space=pl.ANY),
            pl.BlockSpec(memory_space=pl.ANY),
        ],
        out_specs=pl.BlockSpec(memory_space=pl.ANY),
        scratch_shapes=[
            vmem((24, ROWS, 2, T, T), bf16),
            vmem((BLOCKS + 1, T, T), bf16),
            vmem((4 * NC, *chunk), bf16),
            vmem((2, 4 * NC, *chunk), bf16),
            vmem((2 * NC, *chunk), bf16),
            vmem((2 * NC, *chunk), bf16),
            vmem((8, 128), i32),
            vmem((16, 8, 128), i32),
            vmem((32, 128), i32),
            vmem((1, 256), i32),
            vmem((2, 256), i32),
            pltpu.SMEM((1, 256), i32),
            pltpu.SMEM((2, 256), i32),
            pltpu.SMEM((32, 128), i32),
            dma((16, NC)),
            dma((4 * NC,)),
            dma((2, 4 * NC)),
            dma((2 * NC,)),
            dma((2 * NC,)),
            dma((16,)),
            dma((B_PARTS,)),
            dma,
            dma((2,)),
            dma,
            dma,
            dma,
            dma,
            dma,
        ],
        compiler_params=pltpu.CompilerParams(
            collective_id=0, has_side_effects=True, vmem_limit_bytes=63 << 20
        ),
        cost_estimate=pl.CostEstimate(
            flops=2 * 256 * 2 * T * 2 * T * T, bytes_accessed=26 << 20, transcendentals=0
        ),
    )(a_cols.T, b_cols.T, c_cols.T, keep.transpose(2, 1, 0), a_tiles, b_tiles.reshape(BLOCKS, T, T))


def solution(mesh):
    placed = (
        P("col", "row", None, None),
        P("col", "row"),
        P("row", "col", None, None),
        P("row", "col"),
        P(None, "col"),
        P(None, "row", "col"),
    )
    return jax.shard_map(
        per_device,
        mesh=mesh,
        in_specs=placed,
        out_specs=P("row", "col", None, None),
        check_vma=False,
    )
```

```python
import jax
import jax.numpy as jnp
from jax import lax
from jax.experimental import pallas as pl
from jax.experimental.pallas import tpu as pltpu
from jax.sharding import PartitionSpec as P

MESH = pl.DeviceIdType.MESH
T = 128
ROWS = 16
NC = 16
NR = ROWS // NC
KP = 224
SB = 3
BLOCKS = KP * SB
B_PARTS = 8
B_EARLY = 4


def kernel(
    a_cols_ref, b_cols_ref, c_cols_ref, keep_ref, a_ref, b_ref, out_ref,
    w, bv, rf, rd, rz, rzz, mine, land, cols_v, b_words, c_words, b_words_s, c_words_s, cols_s,
    sem_a, sem_f, sem_d, sem_z, sem_zz, sem_m, sem_b, sem_own, sem_words, sem_cols, sem_out, send_a, send_p, send_m,
):
    row, col = lax.axis_index("row"), lax.axis_index("col")
    x, zh = row // 2, row % 2
    y, zl, k = col // 4, (col // 2) % 2, col % 2
    yp, ym, y2 = (y + 1) % 4, (y + 3) % 4, (y + 2) % 4

    def dev(xx, hh, yy, ll, kk):
        return (xx * 2 + hh, yy * 4 + ll * 2 + kk)

    sibling = dev(x, zh, y, zl, 1 - k)
    z_near = dev(x, zh, y, 1 - zl, k)
    z_far = dev(x, 1 - zh, y, zl, k)
    y_up, y_down = dev(x, zh, yp, zl, k), dev(x, zh, ym, zl, k)

    def x_dev(xx):
        return dev(xx, zh, y, zl, k)

    def remote(src, dst, send, recv, device):
        return pltpu.make_async_remote_copy(
            src_ref=src, dst_ref=dst, send_sem=send, recv_sem=recv, device_id=device, device_id_type=MESH
        )

    def landed(dst, recv):
        remote(dst, dst, send_p, recv, sibling).wait_recv()

    def chunk(slot, c):
        return w.at[slot, pl.ds(c * NR, NR)]

    part = BLOCKS // B_PARTS
    b_copies = [
        pltpu.make_async_copy(b_ref.at[pl.ds(i * part, part)], bv.at[pl.ds(i * part, part)], sem_b.at[i])
        for i in range(B_PARTS)
    ]
    q_own = y * 2 + zl
    own_copy = pltpu.make_async_copy(a_ref, w.at[q_own], sem_own)
    own_copy.start()
    for copy in b_copies[:B_EARLY]:
        copy.start()

    barrier = pltpu.get_barrier_semaphore()
    for j in range(1, 16):
        pl.semaphore_signal(barrier, 1, device_id=(row, (col + j) % 16), device_id_type=MESH)
    for device in (x_dev((x + 1) % 4), x_dev((x + 3) % 4), z_far):
        pl.semaphore_signal(barrier, 1, device_id=device, device_id_type=MESH)
    bv[BLOCKS] = jnp.zeros((T, T), bv.dtype)
    mine[...] = jnp.zeros_like(mine)
    mine[0:2, 0:ROWS] = a_cols_ref[...]
    b_words[0:1, 0:KP] = b_cols_ref[0:1] + 128 * b_cols_ref[1:2] + 16384 * b_cols_ref[2:3]
    c_words[...] = (
        c_cols_ref[0:1] + 128 * c_cols_ref[1:2] + 16384 * (keep_ref[0] + 2 * keep_ref[1] + 4 * keep_ref[2])
    )
    words_copies = [
        pltpu.make_async_copy(b_words, b_words_s, sem_words.at[0]),
        pltpu.make_async_copy(c_words, c_words_s, sem_words.at[1]),
    ]
    for copy in words_copies:
        copy.start()
    pl.semaphore_wait(barrier, 18)

    def send_a_chunk(src, slot, c, device):
        remote(src, chunk(slot, c), send_a, sem_a.at[slot, c], device).start()

    def wait_a(slot, c):
        landed(chunk(slot, c), sem_a.at[slot, c])

    def hop0(c):
        src = a_ref.at[pl.ds(c * NR, NR)]
        send_a_chunk(src, q_own, c, y_up)
        send_a_chunk(src, q_own, c, y_down)
        send_a_chunk(src, q_own, c, z_near)
        send_a_chunk(src, 8 + q_own, c, sibling)

    def pass_on(slot, c, up=None, down=None):
        wait_a(slot, c)
        src = chunk(slot, c)
        if up is not None:
            @pl.when(up)
            def _():
                send_a_chunk(src, slot, c, y_up)
        if down is not None:
            @pl.when(down)
            def _():
                send_a_chunk(src, slot, c, y_down)
        send_a_chunk(src, 8 + slot, c, sibling)

    def hop1(c):
        slot = y * 2 + 1 - zl
        pass_on(ym * 2 + zl, c, up=(c + k) % 2 == 0)
        pass_on(yp * 2 + zl, c, down=(c + k) % 2 == 1)
        wait_a(slot, c)
        src = chunk(slot, c)
        send_a_chunk(src, slot, c, y_up)
        send_a_chunk(src, slot, c, y_down)
        send_a_chunk(src, 8 + slot, c, sibling)

    def hop2(c):
        pass_on(ym * 2 + 1 - zl, c, up=(c + k) % 2 == 0)
        pass_on(yp * 2 + 1 - zl, c, down=(c + k) % 2 == 1)
        pass_on(y2 * 2 + zl, c)

    def hop3(c):
        pass_on(y2 * 2 + 1 - zl, c)

    def z_first(c, kk):
        return (c + 2 * kk) % 4 == 0

    def way(c, kk):
        return 1 + 2 * ((c + kk) % 2)

    def p_slot(yy, ll, kk):
        same = 1 - (kk + k) % 2
        return yy * 2 + ll + 8 + 8 * same

    def r_slot(ll, kk, c):
        return (ll * 2 + kk) * NC + c

    def zz_slot(xx, kk, c):
        return (xx * 2 + kk) * 4 + c // 4

    def send_x(xx, ll, kk, c):
        src = chunk(p_slot(xx, ll, kk), c)
        rel = ((xx - x + 4) * way(c, kk)) % 4
        slot = r_slot(ll, kk, c)

        @pl.when(rel == 2)
        def _():
            remote(src, rf.at[slot], send_p, sem_f.at[slot], x_dev((x + way(c, kk)) % 4)).start()

        @pl.when(rel == 3)
        def _():
            remote(src, rd.at[1, slot], send_p, sem_d.at[1, slot], x_dev((x + 4 - way(c, kk)) % 4)).start()

    def add_into(slot, c, *others):
        for r in range(NR):
            for u in range(2):
                total = w[slot, c * NR + r, u].astype(jnp.float32)
                for ref, index in others:
                    total = total + ref[(*index, r, u)].astype(jnp.float32)
                w[slot, c * NR + r, u] = total.astype(w.dtype)

    def multiply(c, *places):
        def one(dk, carry):
            kk = (k + dk) % 2
            slots = [(yy * 2 + ll + 8 * dk, yy * 2 + ll + 16 - 8 * dk) for yy, ll in places]

            @pl.when(dk == 1)
            def _():
                for a_slot, _ in slots:
                    wait_a(a_slot, c)

            rows = [c * NR + r for r in range(NR)]
            found = []
            for yy, ll in places:
                piece = yy * 4 + ll * 2 + kk
                for local in rows:
                    for s in range(2):
                        at = cols_s[16 * s + piece, local]
                        b_word = b_words_s[0, at]
                        c_word = c_words_s[s, piece * ROWS + local]
                        for u in range(2):
                            goal = lax.shift_right_logical(c_word, 7 * u) & 127
                            which = jnp.int32(BLOCKS)
                            for t in range(SB):
                                there = lax.shift_right_logical(b_word, 7 * t) & 127
                                kept = lax.shift_right_logical(c_word, 14 + t) & 1
                                which = jnp.where((there == goal) & (kept == 1), at * SB + t, which)
                            found.append(which)
            products = []
            for a_slot, _ in slots:
                for local in rows:
                    n = 4 * len(products)
                    right = [bv[which] for which in found[n : n + 4]]
                    right = [jnp.concatenate(right[i : i + 2], axis=1) for i in (0, 2)]
                    left = jnp.concatenate([w[a_slot, local, 0], w[a_slot, local, 1]], axis=1)
                    products.append(
                        jnp.dot(left, jnp.concatenate(right, axis=0), preferred_element_type=jnp.float32)
                    )
            for i, (_, out_slot) in enumerate(slots):
                for r, local in enumerate(rows):
                    product = products[i * NR + r]
                    w[out_slot, local, 0] = product[:, :T].astype(w.dtype)
                    w[out_slot, local, 1] = product[:, T:].astype(w.dtype)

            first = z_first(c, kk)

            @pl.when(jnp.logical_not(first))
            def _():
                for yy, ll in places:
                    send_x(yy, ll, kk, c)

            for (yy, ll), (_, out_slot) in zip(places, slots):

                @pl.when(first & (ll != zh))
                def _():
                    slot = zz_slot(yy, kk, c)
                    remote(chunk(out_slot, c), rzz.at[slot], send_p, sem_zz.at[slot], z_far).start()

            return carry

        lax.fori_loop(0, 2, one, 0)

    def z_sum(c):
        for kk in range(2):
            @pl.when(z_first(c, kk))
            def _():
                def one(j, carry):
                    xx = (x + 2 + j) % 4
                    slot = zz_slot(xx, kk, c)
                    landed(rzz.at[slot], sem_zz.at[slot])
                    add_into(p_slot(xx, zh, kk), c, (rzz, (slot,)))
                    send_x(xx, zh, kk, c)
                    return carry

                lax.fori_loop(0, 4, one, 0)

    def middle(c, ll, kk):
        xx = (x + way(c, kk)) % 4
        slot, own = r_slot(ll, kk, c), p_slot(xx, ll, kk)
        landed(rf.at[slot], sem_f.at[slot])
        add_into(own, c, (rf, (slot,)))
        remote(chunk(own, c), rd.at[0, slot], send_p, sem_d.at[0, slot], x_dev(xx)).start()

    def arrived(ll, kk, c):
        slot = r_slot(ll, kk, c)
        for side in range(2):
            landed(rd.at[side, slot], sem_d.at[side, slot])
        return (rd, (0, slot)), (rd, (1, slot))

    def write_out(own, kk, c):
        pltpu.make_async_copy(chunk(own, c), out_ref.at[pl.ds(kk * ROWS + c * NR, NR)], sem_out).start()

    def middles(c, only_z_first):
        for j in range(2):
            ll = (zl + j) % 2
            for kk in range(2):
                if only_z_first:
                    go = z_first(c, kk) & (ll == zh)
                else:
                    go = jnp.logical_not(z_first(c, kk))

                @pl.when(go)
                def _():
                    middle(c, ll, kk)

    def to_far(c):
        for kk in range(2):
            @pl.when(jnp.logical_not(z_first(c, kk)))
            def _():
                own = p_slot(x, 1 - zh, kk)
                add_into(own, c, *arrived(1 - zh, kk, c))
                slot = kk * NC + c
                remote(chunk(own, c), rz.at[slot], send_p, sem_z.at[slot], z_far).start()

    def finish(c):
        for kk in range(2):
            own = p_slot(x, zh, kk)
            slot = kk * NC + c

            @pl.when(z_first(c, kk))
            def _():
                add_into(own, c, *arrived(zh, kk, c))
                write_out(own, kk, c)

            @pl.when(jnp.logical_not(z_first(c, kk)))
            def _():
                both = arrived(zh, kk, c)
                landed(rz.at[slot], sem_z.at[slot])
                add_into(own, c, *both, (rz, (slot,)))
                write_out(own, kk, c)

    for j in range(1, 16):
        remote(mine, land.at[col], send_m, sem_m.at[col], (row, (col + j) % 16)).start()
    hop0(0)
    hop0(1)
    for copy in b_copies[B_EARLY:]:
        copy.start()
    land[col] = mine[...]
    for j in range(1, 16):
        other = (col + j) % 16
        landed(land.at[other], sem_m.at[other])
    for s in range(2):
        cols_v[16 * s : 16 * s + 16] = land[:, s, :]
    cols_copy = pltpu.make_async_copy(cols_v, cols_s, sem_cols)
    cols_copy.start()
    hop1(0)
    for copy in (*words_copies, cols_copy):
        copy.wait()
    own_copy.wait()
    for copy in b_copies:
        copy.wait()

    def during(c, end):
        return pl.when((c >= 0) & (c < end))

    def turn(a, carry):
        @during(a, NC)
        def _():
            multiply(a, (y, zl))

        @during(a + 1, NC)
        def _():
            hop1(a + 1)

        @during(a, NC)
        def _():
            hop2(a)

        @during(a - 1, NC)
        def _():
            hop3(a - 1)

        @during(a + 2, NC)
        def _():
            hop0(a + 2)

        @during(a, NC)
        def _():
            multiply(a, (ym, zl), (yp, zl), (y, 1 - zl))

        @during(a - 2, NC)
        def _():
            z_sum(a - 2)
            middles(a - 2, False)

        @during(a - 3, NC)
        def _():
            middles(a - 3, True)

        @during(a, NC)
        def _():
            multiply(a, (y2, zl), (ym, 1 - zl), (yp, 1 - zl))

        @during(a - 1, NC)
        def _():
            multiply(a - 1, (y2, 1 - zl))

        @during(a - 3, NC)
        def _():
            to_far(a - 3)

        @during(a - 4, NC)
        def _():
            finish(a - 4)

        return carry

    lax.fori_loop(0, NC + 4, turn, 0)

    remote(w.at[pl.ds(0, 15)], w.at[pl.ds(0, 15)], send_a, send_a, sibling).wait_send()
    remote(w.at[pl.ds(0, 14)], w.at[pl.ds(0, 14)], send_p, send_p, sibling).wait_send()
    remote(land.at[pl.ds(0, 15)], land.at[pl.ds(0, 15)], send_m, send_m, sibling).wait_send()
    pltpu.make_async_copy(w.at[pl.ds(0, 2)], w.at[pl.ds(0, 2)], sem_out).wait()


def per_device(a_tiles, a_cols, b_tiles, b_cols, c_cols, keep):
    bf16, i32 = jnp.bfloat16, jnp.int32
    chunk = (NR, 2, T, T)
    vmem = pltpu.VMEM
    dma = pltpu.SemaphoreType.DMA
    return pl.pallas_call(
        kernel,
        out_shape=jax.ShapeDtypeStruct((2 * ROWS, 2, T, T), bf16),
        in_specs=[
            *[pl.BlockSpec(memory_space=pltpu.VMEM)] * 4,
            pl.BlockSpec(memory_space=pl.ANY),
            pl.BlockSpec(memory_space=pl.ANY),
        ],
        out_specs=pl.BlockSpec(memory_space=pl.ANY),
        scratch_shapes=[
            vmem((24, ROWS, 2, T, T), bf16),
            vmem((BLOCKS + 1, T, T), bf16),
            vmem((4 * NC, *chunk), bf16),
            vmem((2, 4 * NC, *chunk), bf16),
            vmem((2 * NC, *chunk), bf16),
            vmem((2 * NC, *chunk), bf16),
            vmem((8, 128), i32),
            vmem((16, 8, 128), i32),
            vmem((32, 128), i32),
            vmem((1, 256), i32),
            vmem((2, 256), i32),
            pltpu.SMEM((1, 256), i32),
            pltpu.SMEM((2, 256), i32),
            pltpu.SMEM((32, 128), i32),
            dma((16, NC)),
            dma((4 * NC,)),
            dma((2, 4 * NC)),
            dma((2 * NC,)),
            dma((2 * NC,)),
            dma((16,)),
            dma((B_PARTS,)),
            dma,
            dma((2,)),
            dma,
            dma,
            dma,
            dma,
            dma,
        ],
        compiler_params=pltpu.CompilerParams(
            collective_id=0, has_side_effects=True, vmem_limit_bytes=63 << 20
        ),
        cost_estimate=pl.CostEstimate(
            flops=2 * 256 * 2 * T * 2 * T * T, bytes_accessed=26 << 20, transcendentals=0
        ),
    )(a_cols.T, b_cols.T, c_cols.T, keep.transpose(2, 1, 0), a_tiles, b_tiles.reshape(BLOCKS, T, T))


def solution(mesh):
    placed = (
        P("col", "row", None, None),
        P("col", "row"),
        P("row", "col", None, None),
        P("row", "col"),
        P(None, "col"),
        P(None, "row", "col"),
    )
    return jax.shard_map(
        per_device,
        mesh=mesh,
        in_specs=placed,
        out_specs=P("row", "col", None, None),
        check_vma=False,
    )
```

```python
import jax
import jax.numpy as jnp
from jax import lax
from jax.experimental import pallas as pl
from jax.experimental.pallas import tpu as pltpu
from jax.sharding import PartitionSpec as P

MESH = pl.DeviceIdType.MESH
T = 128
ROWS = 16
NC = 16
NR = ROWS // NC
KP = 224
SB = 3
BLOCKS = KP * SB
B_PARTS = 8
B_EARLY = 4


def kernel(
    a_cols_ref, b_cols_ref, c_cols_ref, keep_ref, a_ref, b_ref, out_ref, far_ref,
    w, bv, rf, rd, rzz, mine, land, cols_v, b_words, c_words, b_words_s, c_words_s, cols_s,
    sem_a, sem_f, sem_d, sem_z, sem_zz, sem_m, sem_b, sem_own, sem_words, sem_cols, sem_out, sem_zero, send_a, send_p, send_m,
):
    row, col = lax.axis_index("row"), lax.axis_index("col")
    x, zh = row // 2, row % 2
    y, zl, k = col // 4, (col // 2) % 2, col % 2
    yp, ym, y2 = (y + 1) % 4, (y + 3) % 4, (y + 2) % 4

    def dev(xx, hh, yy, ll, kk):
        return (xx * 2 + hh, yy * 4 + ll * 2 + kk)

    sibling = dev(x, zh, y, zl, 1 - k)
    z_near = dev(x, zh, y, 1 - zl, k)
    z_far = dev(x, 1 - zh, y, zl, k)
    y_up, y_down = dev(x, zh, yp, zl, k), dev(x, zh, ym, zl, k)

    def x_dev(xx):
        return dev(xx, zh, y, zl, k)

    def remote(src, dst, send, recv, device):
        return pltpu.make_async_remote_copy(
            src_ref=src, dst_ref=dst, send_sem=send, recv_sem=recv, device_id=device, device_id_type=MESH
        )

    def landed(dst, recv):
        remote(dst, dst, send_p, recv, sibling).wait_recv()

    def chunk(slot, c):
        return w.at[slot, pl.ds(c * NR, NR)]

    part = BLOCKS // B_PARTS
    b_copies = [
        pltpu.make_async_copy(b_ref.at[pl.ds(i * part, part)], bv.at[pl.ds(i * part, part)], sem_b.at[i])
        for i in range(B_PARTS)
    ]
    q_own = y * 2 + zl
    own_copy = pltpu.make_async_copy(a_ref, w.at[q_own], sem_own)
    own_copy.start()
    for copy in b_copies[:B_EARLY]:
        copy.start()

    barrier = pltpu.get_barrier_semaphore()
    for j in range(1, 16):
        pl.semaphore_signal(barrier, 1, device_id=(row, (col + j) % 16), device_id_type=MESH)
    for device in (x_dev((x + 1) % 4), x_dev((x + 3) % 4), z_far):
        pl.semaphore_signal(barrier, 1, device_id=device, device_id_type=MESH)
    bv[BLOCKS] = jnp.zeros((T, T), bv.dtype)
    mine[...] = jnp.zeros_like(mine)
    mine[0:2, 0:ROWS] = a_cols_ref[...]
    b_words[0:1, 0:KP] = b_cols_ref[0:1] + 128 * b_cols_ref[1:2] + 16384 * b_cols_ref[2:3]
    c_words[...] = (
        c_cols_ref[0:1] + 128 * c_cols_ref[1:2] + 16384 * (keep_ref[0] + 2 * keep_ref[1] + 4 * keep_ref[2])
    )
    words_copies = [
        pltpu.make_async_copy(b_words, b_words_s, sem_words.at[0]),
        pltpu.make_async_copy(c_words, c_words_s, sem_words.at[1]),
    ]
    for copy in words_copies:
        copy.start()
    pl.semaphore_wait(barrier, 18)

    def send_a_chunk(src, slot, c, device):
        remote(src, chunk(slot, c), send_a, sem_a.at[slot, c], device).start()

    def wait_a(slot, c):
        landed(chunk(slot, c), sem_a.at[slot, c])

    def hop0(c):
        src = a_ref.at[pl.ds(c * NR, NR)]
        send_a_chunk(src, q_own, c, y_up)
        send_a_chunk(src, q_own, c, y_down)
        send_a_chunk(src, q_own, c, z_near)
        send_a_chunk(src, 8 + q_own, c, sibling)

    def pass_on(slot, c, up=None, down=None):
        wait_a(slot, c)
        src = chunk(slot, c)
        if up is not None:
            @pl.when(up)
            def _():
                send_a_chunk(src, slot, c, y_up)
        if down is not None:
            @pl.when(down)
            def _():
                send_a_chunk(src, slot, c, y_down)
        send_a_chunk(src, 8 + slot, c, sibling)

    def hop1(c):
        slot = y * 2 + 1 - zl
        pass_on(ym * 2 + zl, c, up=(c + k) % 2 == 0)
        pass_on(yp * 2 + zl, c, down=(c + k) % 2 == 1)
        wait_a(slot, c)
        src = chunk(slot, c)
        send_a_chunk(src, slot, c, y_up)
        send_a_chunk(src, slot, c, y_down)
        send_a_chunk(src, 8 + slot, c, sibling)

    def hop2(c):
        pass_on(ym * 2 + 1 - zl, c, up=(c + k) % 2 == 0)
        pass_on(yp * 2 + 1 - zl, c, down=(c + k) % 2 == 1)
        pass_on(y2 * 2 + zl, c)

    def hop3(c):
        pass_on(y2 * 2 + 1 - zl, c)

    def z_first(c, kk):
        return (c + 2 * kk) % 4 == 0

    def way(c, kk):
        return 1 + 2 * ((c + kk) % 2)

    def p_slot(yy, ll, kk):
        same = 1 - (kk + k) % 2
        return yy * 2 + ll + 8 + 8 * same

    def r_slot(ll, kk, c):
        return (ll * 2 + kk) * NC + c

    def zz_slot(xx, kk, c):
        return (xx * 2 + kk) * 4 + c // 4

    def send_x(xx, ll, kk, c):
        src = chunk(p_slot(xx, ll, kk), c)
        rel = ((xx - x + 4) * way(c, kk)) % 4
        slot = r_slot(ll, kk, c)

        @pl.when(rel == 2)
        def _():
            remote(src, rf.at[slot], send_p, sem_f.at[slot], x_dev((x + way(c, kk)) % 4)).start()

        @pl.when(rel == 3)
        def _():
            remote(src, rd.at[1, slot], send_p, sem_d.at[1, slot], x_dev((x + 4 - way(c, kk)) % 4)).start()

    def add_into(slot, c, *others):
        for r in range(NR):
            for u in range(2):
                total = w[slot, c * NR + r, u].astype(jnp.float32)
                for ref, index in others:
                    total = total + ref[(*index, r, u)].astype(jnp.float32)
                w[slot, c * NR + r, u] = total.astype(w.dtype)

    def multiply(c, *places):
        def one(dk, carry):
            kk = (k + dk) % 2
            slots = [(yy * 2 + ll + 8 * dk, yy * 2 + ll + 16 - 8 * dk) for yy, ll in places]

            @pl.when(dk == 1)
            def _():
                for a_slot, _ in slots:
                    wait_a(a_slot, c)

            rows = [c * NR + r for r in range(NR)]
            found = []
            for yy, ll in places:
                piece = yy * 4 + ll * 2 + kk
                for local in rows:
                    for s in range(2):
                        at = cols_s[16 * s + piece, local]
                        b_word = b_words_s[0, at]
                        c_word = c_words_s[s, piece * ROWS + local]
                        for u in range(2):
                            goal = lax.shift_right_logical(c_word, 7 * u) & 127
                            which = jnp.int32(BLOCKS)
                            for t in range(SB):
                                there = lax.shift_right_logical(b_word, 7 * t) & 127
                                kept = lax.shift_right_logical(c_word, 14 + t) & 1
                                which = jnp.where((there == goal) & (kept == 1), at * SB + t, which)
                            found.append(which)
            products = []
            for a_slot, _ in slots:
                for local in rows:
                    n = 4 * len(products)
                    right = [bv[which] for which in found[n : n + 4]]
                    right = [jnp.concatenate(right[i : i + 2], axis=1) for i in (0, 2)]
                    left = jnp.concatenate([w[a_slot, local, 0], w[a_slot, local, 1]], axis=1)
                    products.append(
                        jnp.dot(left, jnp.concatenate(right, axis=0), preferred_element_type=jnp.float32)
                    )
            for i, (_, out_slot) in enumerate(slots):
                for r, local in enumerate(rows):
                    product = products[i * NR + r]
                    w[out_slot, local, 0] = product[:, :T].astype(w.dtype)
                    w[out_slot, local, 1] = product[:, T:].astype(w.dtype)

            first = z_first(c, kk)

            @pl.when(jnp.logical_not(first))
            def _():
                for yy, ll in places:
                    send_x(yy, ll, kk, c)

            for (yy, ll), (_, out_slot) in zip(places, slots):

                @pl.when(first & (ll != zh))
                def _():
                    slot = zz_slot(yy, kk, c)
                    remote(chunk(out_slot, c), rzz.at[slot], send_p, sem_zz.at[slot], z_far).start()

            return carry

        lax.fori_loop(0, 2, one, 0)

    def z_sum(c):
        for kk in range(2):
            @pl.when(z_first(c, kk))
            def _():
                def one(j, carry):
                    xx = (x + 2 + j) % 4
                    slot = zz_slot(xx, kk, c)
                    landed(rzz.at[slot], sem_zz.at[slot])
                    add_into(p_slot(xx, zh, kk), c, (rzz, (slot,)))
                    send_x(xx, zh, kk, c)
                    return carry

                lax.fori_loop(0, 4, one, 0)

    def middle(c, ll, kk):
        xx = (x + way(c, kk)) % 4
        slot, own = r_slot(ll, kk, c), p_slot(xx, ll, kk)
        landed(rf.at[slot], sem_f.at[slot])
        add_into(own, c, (rf, (slot,)))
        remote(chunk(own, c), rd.at[0, slot], send_p, sem_d.at[0, slot], x_dev(xx)).start()

    def arrived(ll, kk, c):
        slot = r_slot(ll, kk, c)
        for side in range(2):
            landed(rd.at[side, slot], sem_d.at[side, slot])
        return (rd, (0, slot)), (rd, (1, slot))

    def result_rows(ref, kk, c):
        return ref.at[pl.ds(kk * ROWS + c * NR, NR)]

    def middles(c, only_z_first):
        for j in range(2):
            ll = (zl + j) % 2
            for kk in range(2):
                if only_z_first:
                    go = z_first(c, kk) & (ll == zh)
                else:
                    go = jnp.logical_not(z_first(c, kk))

                @pl.when(go)
                def _():
                    middle(c, ll, kk)

    def to_far(c):
        for kk in range(2):
            @pl.when(jnp.logical_not(z_first(c, kk)))
            def _():
                own = p_slot(x, 1 - zh, kk)
                add_into(own, c, *arrived(1 - zh, kk, c))
                slot = kk * NC + c
                remote(chunk(own, c), result_rows(far_ref, kk, c), send_p, sem_z.at[slot], z_far).start()

    def finish(c):
        for kk in range(2):
            own = p_slot(x, zh, kk)
            add_into(own, c, *arrived(zh, kk, c))
            pltpu.make_async_copy(chunk(own, c), result_rows(out_ref, kk, c), sem_out).start()

            @pl.when(z_first(c, kk))
            def _():
                for r in range(NR):
                    for u in range(2):
                        to = far_ref.at[kk * ROWS + c * NR + r, pl.ds(u, 1)]
                        pltpu.make_async_copy(bv.at[pl.ds(BLOCKS, 1)], to, sem_zero).start()

    def far_landed(c):
        for kk in range(2):
            @pl.when(jnp.logical_not(z_first(c, kk)))
            def _():
                landed(result_rows(far_ref, kk, c), sem_z.at[kk * NC + c])

    for j in range(1, 16):
        remote(mine, land.at[col], send_m, sem_m.at[col], (row, (col + j) % 16)).start()
    hop0(0)
    hop0(1)
    for copy in b_copies[B_EARLY:]:
        copy.start()
    land[col] = mine[...]
    for j in range(1, 16):
        other = (col + j) % 16
        landed(land.at[other], sem_m.at[other])
    for s in range(2):
        cols_v[16 * s : 16 * s + 16] = land[:, s, :]
    cols_copy = pltpu.make_async_copy(cols_v, cols_s, sem_cols)
    cols_copy.start()
    hop1(0)
    for copy in (*words_copies, cols_copy):
        copy.wait()
    own_copy.wait()
    for copy in b_copies:
        copy.wait()

    def during(c, end):
        return pl.when((c >= 0) & (c < end))

    def turn(a, carry):
        @during(a, NC)
        def _():
            multiply(a, (y, zl))

        @during(a + 1, NC)
        def _():
            hop1(a + 1)

        @during(a, NC)
        def _():
            hop2(a)

        @during(a - 1, NC)
        def _():
            hop3(a - 1)

        @during(a + 2, NC)
        def _():
            hop0(a + 2)

        @during(a, NC)
        def _():
            multiply(a, (ym, zl), (yp, zl), (y, 1 - zl))

        @during(a - 2, NC)
        def _():
            z_sum(a - 2)
            middles(a - 2, False)

        @during(a - 3, NC)
        def _():
            middles(a - 3, True)

        @during(a, NC)
        def _():
            multiply(a, (y2, zl), (ym, 1 - zl), (yp, 1 - zl))

        @during(a - 1, NC)
        def _():
            multiply(a - 1, (y2, 1 - zl))

        @during(a - 3, NC)
        def _():
            to_far(a - 3)

        @during(a - 4, NC)
        def _():
            finish(a - 4)
            far_landed(a - 4)

        return carry

    lax.fori_loop(0, NC + 4, turn, 0)

    remote(w.at[pl.ds(0, 15)], w.at[pl.ds(0, 15)], send_a, send_a, sibling).wait_send()
    remote(w.at[pl.ds(0, 14)], w.at[pl.ds(0, 14)], send_p, send_p, sibling).wait_send()
    remote(land.at[pl.ds(0, 15)], land.at[pl.ds(0, 15)], send_m, send_m, sibling).wait_send()
    pltpu.make_async_copy(w.at[pl.ds(0, 2)], w.at[pl.ds(0, 2)], sem_out).wait()
    zeros = w.at[0, pl.ds(0, 8 * NR)]
    pltpu.make_async_copy(zeros, zeros, sem_zero).wait()


def per_device(a_tiles, a_cols, b_tiles, b_cols, c_cols, keep):
    bf16, i32 = jnp.bfloat16, jnp.int32
    chunk = (NR, 2, T, T)
    vmem = pltpu.VMEM
    dma = pltpu.SemaphoreType.DMA
    own, far = pl.pallas_call(
        kernel,
        out_shape=[jax.ShapeDtypeStruct((2 * ROWS, 2, T, T), bf16)] * 2,
        in_specs=[
            *[pl.BlockSpec(memory_space=pltpu.VMEM)] * 4,
            pl.BlockSpec(memory_space=pl.ANY),
            pl.BlockSpec(memory_space=pl.ANY),
        ],
        out_specs=[pl.BlockSpec(memory_space=pl.ANY)] * 2,
        scratch_shapes=[
            vmem((24, ROWS, 2, T, T), bf16),
            vmem((BLOCKS + 1, T, T), bf16),
            vmem((4 * NC, *chunk), bf16),
            vmem((2, 4 * NC, *chunk), bf16),
            vmem((2 * NC, *chunk), bf16),
            vmem((8, 128), i32),
            vmem((16, 8, 128), i32),
            vmem((32, 128), i32),
            vmem((1, 256), i32),
            vmem((2, 256), i32),
            pltpu.SMEM((1, 256), i32),
            pltpu.SMEM((2, 256), i32),
            pltpu.SMEM((32, 128), i32),
            dma((16, NC)),
            dma((4 * NC,)),
            dma((2, 4 * NC)),
            dma((2 * NC,)),
            dma((2 * NC,)),
            dma((16,)),
            dma((B_PARTS,)),
            dma,
            dma((2,)),
            dma,
            dma,
            dma,
            dma,
            dma,
            dma,
        ],
        compiler_params=pltpu.CompilerParams(
            collective_id=0, has_side_effects=True, vmem_limit_bytes=63 << 20
        ),
        cost_estimate=pl.CostEstimate(
            flops=2 * 256 * 2 * T * 2 * T * T, bytes_accessed=26 << 20, transcendentals=0
        ),
    )(a_cols.T, b_cols.T, c_cols.T, keep.transpose(2, 1, 0), a_tiles, b_tiles.reshape(BLOCKS, T, T))
    return (own.astype(jnp.float32) + far.astype(jnp.float32)).astype(bf16)


def solution(mesh):
    placed = (
        P("col", "row", None, None),
        P("col", "row"),
        P("row", "col", None, None),
        P("row", "col"),
        P(None, "col"),
        P(None, "row", "col"),
    )
    return jax.shard_map(
        per_device,
        mesh=mesh,
        in_specs=placed,
        out_specs=P("row", "col", None, None),
        check_vma=False,
    )
```
